32 devices in a mesh: grp: 2 (over x), row: 16 (over z, y, core).
Axes of the slice: x: 2, y: 2, z: 4, core: 2. Of those that a mesh axis runs over, the one named last changes fastest.
Arguments:
- sequence_features: bfloat16 [256, 128, 64], P('grp', 'row'), parts along dimension 0, may hold values from -6 to 6
- edge_features: bfloat16 [256, 128, 128], P(('grp', 'row')), parts along dimension 0, may hold values from -6 to 6
- residue_features: bfloat16 [256, 384], P(('grp', 'row')), parts along dimension 0, may hold values from -6 to 6
- polymer_labels: int32 [256], P('grp'), parts along dimension 0, may hold values from 0 to 7, never falling along the last dimension, each value on 1 to 64 neighbouring positions
- polymer_membership: int32 [16, 128], P('grp'), parts along dimension 0, may hold values from 0 to 1, as said below
- present_residue_flags: int32 [256], P('grp'), parts along dimension 0, may hold values 0 or 1
- sequence_scaling_vector: float32 [64], replicated, may hold values from 0.1 to 1.9
- first_embedding_matrix: bfloat16 [64, 32], replicated, may hold values from -0.75 to 0.75
- second_embedding_matrix: bfloat16 [64, 32], replicated, may hold values from -0.75 to 0.75
- contraction_matrix: bfloat16 [1024, 128], replicated, may hold values from -0.375 to 0.375
- contraction_offset: float32 [128], replicated, may hold values from -3 to 3
- feedforward_scaling_vector: float32 [128], replicated, may hold values from 0.1 to 1.9
- feedforward_switch_matrix: bfloat16 [128, 512], replicated, may hold values from -0.5 to 0.5
- widening_matrix: bfloat16 [128, 512], replicated, may hold values from -0.5 to 0.5
- narrowing_matrix: bfloat16 [512, 128], replicated, may hold values from -0.25 to 0.25
- logit_scaling_vector: float32 [128], replicated, may hold values from 0.1 to 1.9
- edge_logit_matrix: bfloat16 [128, 16], replicated, may hold values from -2 to 2
- residue_scaling_vector: float32 [384], replicated, may hold values from 0.1 to 1.9
- asking_matrix: bfloat16 [384, 384], replicated, as said below
- lookup_matrix: bfloat16 [384, 384], replicated, as said below
- content_matrix: bfloat16 [384, 384], replicated, may hold values from -0.3125 to 0.3125
- heads_sigmoid_matrix: bfloat16 [384, 384], replicated, may hold values from -0.3125 to 0.3125
- heads_merge_matrix: bfloat16 [384, 384], replicated, may hold values from -0.3125 to 0.3125
Outputs:
- pair_out: bfloat16 [256, 128, 128], P(('grp', 'row')), parts along dimension 0
- single_out: bfloat16 [256, 384], P(('grp', 'row')), parts along dimension 0
The draws below stay inside these ranges and needn't reach their ends.
There are 2 independent parts, one for each index of `grp`. The reference program is written for one: setup_inputs(seed, part) draws one part's arguments, and reference() takes and returns one part's arrays. A program takes and returns all parts, laid end to end along the dimension named above; an argument that names none is the same for every part. Nothing has to cross between parts.
Inputs may be any that keep to these rules, and one draw needn't show every extreme that they name: `polymer_labels`: never falling along the tokens. `polymer_membership`: entry [c, s] is 1 where chain c takes part in MSA row s; every chain takes part in exactly 64 rows. `present_residue_flags`: 1 marks a real token. `asking_matrix`: a real matrix. `lookup_matrix`: a real matrix.
All inputs are finite; a program needn't handle non-finite values.
Results may differ from the reference program's by a relative error of at most 0.012.
Values may be sent and summed in bfloat16 or wider, within the bound.
A program may use at most 128 MiB of HBM per device.

```python
import math
import jax
import jax.numpy as jnp
import numpy as np
from jax import lax

SEQUENCE_DEPTH = 64
FEATURE_SIZE = 32
CZ = 128
HID = 512
CS = 384
HEADS = 16
SEQUENCE_TOTAL = 128
CHAINS = 8
RESIDUE_TOTAL = 128
HEAD_DIM = 24


def projection_pair(key):
    offset_begin = jax.random.fold_in(key, 7301)
    first, second = jax.random.split(offset_begin)
    scaled = jnp.sqrt(jnp.float32(CS))
    keys = jax.random.normal(first, (CS, CS), jnp.float32) / scaled
    queries = jax.random.normal(second, (CS, CS), jnp.float32) / scaled
    return (queries, keys)


def draw_asking_matrix(key, part):
    return projection_pair(key)[0].astype(jnp.bfloat16)


def draw_lookup_matrix(key, part):
    return projection_pair(key)[1].astype(jnp.bfloat16)


def draw_polymer_membership(key, part):
    offset_begin = jax.random.fold_in(key, 4409)
    participants = []
    for polymer in range(CHAINS - 1):
        sorting_permutation = jax.random.permutation(jax.random.fold_in(offset_begin, polymer), SEQUENCE_TOTAL)
        position = jnp.argsort(sorting_permutation)
        participants.append((position < SEQUENCE_TOTAL // 2).astype(jnp.int32))
    participants.append(1 - participants[0])
    return jnp.stack(participants, axis=0).astype(jnp.int32)


def set_ends(values, stream_key, least, top_value):
    shape = values.shape
    index_at = [jax.random.randint(jax.random.fold_in(stream_key, axis), (), 0, shape[axis]) for axis in range(len(shape))]
    values = values.at[tuple(index_at)].set(least)
    longest = shape.index(max(shape))
    index_at[longest] = (index_at[longest] + 1) % shape[longest]
    return values.at[tuple(index_at)].set(top_value)


def block_scale(key, extent, pieces, least, high):
    factor_of, own = 1.0, jax.random.fold_in(key, 6)
    for dim, blocks in pieces:
        steps = jnp.exp(jax.random.uniform(jax.random.fold_in(own, dim), (blocks,), jnp.float32, least / len(pieces), high / len(pieces)))
        factor_of = factor_of * jnp.repeat(steps, extent[dim] // blocks).reshape([-1 if axis == dim else 1 for axis in range(len(extent))])
    return factor_of


def length_profile(amount, total, reach, slope):
    portions = [(1 << 20) // math.isqrt(rank ** slope) + 1 for rank in range(2, amount + 1)]
    surplus, holding = total - reach - (amount - 1), [1] * (amount - 1)
    while surplus > 0:
        candidates = [i for i in range(amount - 1) if holding[i] < reach]
        pool, budget = sum([portions[i] for i in candidates]), surplus
        for i in candidates:
            more = min(reach - holding[i], max(1, budget * portions[i] // pool), surplus)
            holding[i] = holding[i] + more
            surplus = surplus - more
    return np.array([reach] + holding)


def ragged(rng, amount, total, bound, lean):
    if amount == 2:
        one = jax.random.randint(rng, (), max(1, total - bound), min(bound, total - 1) + 1)
        return jnp.stack([one, total - one])
    lengths = jnp.asarray(length_profile(amount, total, bound, lean), jnp.int32)
    twos = (amount - 1) // 2
    giver, receiver = lengths[1:1 + 2 * twos:2], lengths[2:2 + 2 * twos:2]
    margin = jnp.minimum(giver - 1, bound - receiver)
    moved = jax.random.randint(jax.random.fold_in(rng, 1), (twos,), 0, 1 << 20) % (margin + 1)
    lengths = lengths.at[1:1 + 2 * twos:2].set(giver - moved).at[2:2 + 2 * twos:2].set(receiver + moved)
    return lengths[jax.random.permutation(jax.random.fold_in(rng, 2), amount)]


def gaussian(stream_key, dims, scale, most, shards=(), kind=jnp.bfloat16):
    level = block_scale(stream_key, dims, shards, -0.22, 0.18) if shards else 1.0
    drawn = jax.random.normal(stream_key, dims, jnp.float32) * scale * level
    return jnp.minimum(jnp.maximum(drawn, -most), most).astype(kind)


def setup_inputs(seed: int = 0, part: int = 0) -> dict:
    arg_keys = jax.random.split(jax.random.key(seed), 24)
    part_splits = jax.random.split(jax.random.fold_in(arg_keys[23], part), 24)
    sequence_features = gaussian(part_splits[0], (SEQUENCE_TOTAL, RESIDUE_TOTAL, SEQUENCE_DEPTH), 1.0, 6.0, ((1, 16),))
    edge_features = gaussian(part_splits[1], (RESIDUE_TOTAL, RESIDUE_TOTAL, CZ), 1.0, 6.0, ((0, 16),))
    residue_features = gaussian(part_splits[2], (RESIDUE_TOTAL, CS), 1.0, 6.0, ((0, 16),))
    polymer_labels = jnp.searchsorted(jnp.cumsum(ragged(part_splits[3], CHAINS, RESIDUE_TOTAL, RESIDUE_TOTAL // 2, 2)), jnp.arange(RESIDUE_TOTAL), side="right").astype(jnp.int32)
    polymer_membership = draw_polymer_membership(jax.random.fold_in(jax.random.fold_in(arg_keys[23], part), 71), part)
    present_residue_flags = set_ends((jax.random.randint(part_splits[5], (RESIDUE_TOTAL,), 0, 8) < 7).astype(jnp.int32), jax.random.fold_in(part_splits[5], 1), 0, 1)
    sequence_scaling_vector = jnp.clip(1.0 + 0.18 * jax.random.normal(arg_keys[6], (SEQUENCE_DEPTH,), jnp.float32), 0.1, 1.9)
    first_embedding_matrix = gaussian(arg_keys[7], (SEQUENCE_DEPTH, FEATURE_SIZE), SEQUENCE_DEPTH ** -0.5, 0.75)
    second_embedding_matrix = gaussian(arg_keys[8], (SEQUENCE_DEPTH, FEATURE_SIZE), SEQUENCE_DEPTH ** -0.5, 0.75)
    contraction_matrix = gaussian(arg_keys[9], (FEATURE_SIZE * FEATURE_SIZE, CZ), (FEATURE_SIZE * FEATURE_SIZE // 4) ** -0.5, 0.375)
    contraction_offset = gaussian(arg_keys[10], (CZ,), 0.5, 3.0, (), jnp.float32)
    feedforward_scaling_vector = jnp.clip(1.0 + 0.18 * jax.random.normal(arg_keys[11], (CZ,), jnp.float32), 0.1, 1.9)
    feedforward_switch_matrix = gaussian(arg_keys[12], (CZ, HID), CZ ** -0.5, 0.5)
    widening_matrix = gaussian(arg_keys[13], (CZ, HID), CZ ** -0.5, 0.5)
    narrowing_matrix = gaussian(arg_keys[14], (HID, CZ), HID ** -0.5, 0.25)
    logit_scaling_vector = jnp.clip(1.0 + 0.18 * jax.random.normal(arg_keys[15], (CZ,), jnp.float32), 0.1, 1.9)
    edge_logit_matrix = gaussian(arg_keys[16], (CZ, HEADS), (CZ // 16) ** -0.5, 2.0)
    residue_scaling_vector = jnp.clip(1.0 + 0.18 * jax.random.normal(arg_keys[17], (CS,), jnp.float32), 0.1, 1.9)
    asking_matrix = draw_asking_matrix(jax.random.fold_in(arg_keys[23], 71), part)
    lookup_matrix = draw_lookup_matrix(jax.random.fold_in(arg_keys[23], 71), part)
    content_matrix = gaussian(arg_keys[20], (CS, CS), CS ** -0.5, 0.3125)
    heads_sigmoid_matrix = gaussian(arg_keys[21], (CS, CS), CS ** -0.5, 0.3125)
    heads_merge_matrix = gaussian(arg_keys[22], (CS, CS), CS ** -0.5, 0.3125)
    return {"sequence_features": sequence_features, "edge_features": edge_features, "residue_features": residue_features, "polymer_labels": polymer_labels, "polymer_membership": polymer_membership, "present_residue_flags": present_residue_flags, "sequence_scaling_vector": sequence_scaling_vector, "first_embedding_matrix": first_embedding_matrix, "second_embedding_matrix": second_embedding_matrix, "contraction_matrix": contraction_matrix, "contraction_offset": contraction_offset, "feedforward_scaling_vector": feedforward_scaling_vector, "feedforward_switch_matrix": feedforward_switch_matrix, "widening_matrix": widening_matrix, "narrowing_matrix": narrowing_matrix, "logit_scaling_vector": logit_scaling_vector, "edge_logit_matrix": edge_logit_matrix, "residue_scaling_vector": residue_scaling_vector, "asking_matrix": asking_matrix, "lookup_matrix": lookup_matrix, "content_matrix": content_matrix, "heads_sigmoid_matrix": heads_sigmoid_matrix, "heads_merge_matrix": heads_merge_matrix}


epsilon = 1e-05
highest = lax.Precision.HIGHEST

def standardize_features(values, scales):
    values = values.astype(jnp.float32)
    centred = values - lax.optimization_barrier(jnp.mean(values, axis=-1, keepdims=True))
    spread = lax.optimization_barrier(jnp.mean(centred * centred, axis=-1, keepdims=True))
    return centred * lax.rsqrt(spread + epsilon) * scales

def reference(sequence_features, edge_features, residue_features, polymer_labels, polymer_membership, present_residue_flags, sequence_scaling_vector, first_embedding_matrix, second_embedding_matrix, contraction_matrix, contraction_offset, feedforward_scaling_vector, feedforward_switch_matrix, widening_matrix, narrowing_matrix, logit_scaling_vector, edge_logit_matrix, residue_scaling_vector, asking_matrix, lookup_matrix, content_matrix, heads_sigmoid_matrix, heads_merge_matrix):
    onehot = (polymer_labels[:, None] == jnp.arange(CHAINS, dtype=jnp.int32)[None, :]).astype(jnp.float32)
    pair_rows = polymer_membership.astype(jnp.float32)
    sequence_present_flags = jnp.dot(onehot, pair_rows, precision=highest).T
    shared = jnp.dot(pair_rows, pair_rows.T, precision=highest)
    counts = jnp.dot(jnp.dot(onehot, shared, precision=highest), onehot.T, precision=highest)
    standardized_sequences = standardize_features(sequence_features, sequence_scaling_vector).astype(jnp.bfloat16).reshape(SEQUENCE_TOTAL * RESIDUE_TOTAL, SEQUENCE_DEPTH)
    first_embedding_entries = (jnp.dot(standardized_sequences, first_embedding_matrix, preferred_element_type=jnp.float32).reshape(SEQUENCE_TOTAL, RESIDUE_TOTAL, FEATURE_SIZE) * sequence_present_flags[:, :, None]).astype(jnp.bfloat16)
    second_embedding_entries = (jnp.dot(standardized_sequences, second_embedding_matrix, preferred_element_type=jnp.float32).reshape(SEQUENCE_TOTAL, RESIDUE_TOTAL, FEATURE_SIZE) * sequence_present_flags[:, :, None]).astype(jnp.bfloat16)
    second_merged = second_embedding_entries.reshape(SEQUENCE_TOTAL, RESIDUE_TOTAL * FEATURE_SIZE)
    sequence_group = min(16, RESIDUE_TOTAL)

    def pair_block(beginning):
        first_sequences = lax.dynamic_slice_in_dim(first_embedding_entries, beginning, sequence_group, 1).reshape(SEQUENCE_TOTAL, sequence_group * FEATURE_SIZE)
        outer = lax.dot_general(first_sequences, second_merged, (((0,), (0,)), ((), ())), preferred_element_type=jnp.float32)
        outer = outer.reshape(sequence_group, FEATURE_SIZE, RESIDUE_TOTAL, FEATURE_SIZE).transpose(0, 2, 1, 3).reshape(sequence_group, RESIDUE_TOTAL, FEATURE_SIZE * FEATURE_SIZE)
        shared_rows = lax.dynamic_slice_in_dim(counts, beginning, sequence_group, 0)
        outer = (outer / jnp.maximum(shared_rows, 1.0)[:, :, None]).astype(jnp.bfloat16)
        update = jnp.dot(outer.reshape(sequence_group * RESIDUE_TOTAL, FEATURE_SIZE * FEATURE_SIZE), contraction_matrix, preferred_element_type=jnp.float32) + contraction_offset
        old_rows = lax.dynamic_slice_in_dim(edge_features, beginning, sequence_group, 0).reshape(sequence_group * RESIDUE_TOTAL, CZ)
        pair_one = (old_rows.astype(jnp.float32) + update).astype(jnp.bfloat16)
        normed_pair = standardize_features(pair_one, feedforward_scaling_vector).astype(jnp.bfloat16)
        gated = jnp.dot(normed_pair, feedforward_switch_matrix, preferred_element_type=jnp.float32)
        lifted = jnp.dot(normed_pair, widening_matrix, preferred_element_type=jnp.float32)
        hidden = (jax.nn.silu(gated) * lifted).astype(jnp.bfloat16)
        pair_two = (pair_one.astype(jnp.float32) + jnp.dot(hidden, narrowing_matrix, preferred_element_type=jnp.float32)).astype(jnp.bfloat16)
        bias_normed = standardize_features(pair_two, logit_scaling_vector).astype(jnp.bfloat16)
        bias_rows = jnp.dot(bias_normed, edge_logit_matrix, preferred_element_type=jnp.float32)
        return (pair_two.reshape(sequence_group, RESIDUE_TOTAL, CZ), bias_rows.reshape(sequence_group, RESIDUE_TOTAL, HEADS))
    starts = jnp.arange(0, RESIDUE_TOTAL, sequence_group, dtype=jnp.int32)
    pair_out, bias_all = lax.map(pair_block, starts)
    pair_out = pair_out.reshape(RESIDUE_TOTAL, RESIDUE_TOTAL, CZ)
    bias_all = bias_all.reshape(RESIDUE_TOTAL, RESIDUE_TOTAL, HEADS)
    normed_single = standardize_features(residue_features, residue_scaling_vector).astype(jnp.bfloat16)
    query = jnp.dot(normed_single, asking_matrix, preferred_element_type=jnp.float32).astype(jnp.bfloat16)
    keys = jnp.dot(normed_single, lookup_matrix, preferred_element_type=jnp.float32).astype(jnp.bfloat16)
    values = jnp.dot(normed_single, content_matrix, preferred_element_type=jnp.float32).astype(jnp.bfloat16)
    sigmoid_gate = jax.nn.sigmoid(jnp.dot(normed_single, heads_sigmoid_matrix, preferred_element_type=jnp.float32))
    query_heads = query.astype(jnp.float32).reshape(RESIDUE_TOTAL, HEADS, HEAD_DIM)
    key_heads = keys.astype(jnp.float32).reshape(RESIDUE_TOTAL, HEADS, HEAD_DIM)
    value_heads = values.astype(jnp.float32).reshape(RESIDUE_TOTAL, HEADS, HEAD_DIM)
    scores = jnp.einsum('ihd,jhd->hij', query_heads, key_heads) / math.sqrt(HEAD_DIM) + bias_all.transpose(2, 0, 1)
    live = (present_residue_flags == 1)[None, None, :]
    scores = jnp.where(live, scores, -1e+30)
    peaks = lax.optimization_barrier(jnp.max(scores, axis=-1, keepdims=True))
    expos = jnp.where(live, jnp.exp(scores - peaks), 0.0)
    totals = lax.optimization_barrier(jnp.sum(expos, axis=-1))
    weights = expos.astype(jnp.bfloat16)
    mixed = jnp.einsum('hij,jhd->ihd', weights.astype(jnp.float32), value_heads) / totals.T[:, :, None]
    attended = (mixed.reshape(RESIDUE_TOTAL, CS) * sigmoid_gate).astype(jnp.bfloat16)
    single_out = (residue_features.astype(jnp.float32) + jnp.dot(attended, heads_merge_matrix, preferred_element_type=jnp.float32)).astype(jnp.bfloat16)
    return (pair_out, single_out)
```

```python
import functools
import math

import jax
import jax.numpy as jnp
from jax import lax
from jax.experimental import pallas as pl
from jax.experimental.pallas import tpu as pltpu
from jax.sharding import PartitionSpec as P

epsilon = 1e-05
highest = lax.Precision.HIGHEST
F32 = jnp.float32
BF16 = jnp.bfloat16


def standardize_features(values, scales):
    values = values.astype(F32)
    centred = values - jnp.mean(values, axis=-1, keepdims=True)
    spread = jnp.mean(centred * centred, axis=-1, keepdims=True)
    return centred * lax.rsqrt(spread + epsilon) * scales


def digits(count):
    core = 2 if count % 2 == 0 else 1
    chips = count // core
    fast = 1
    while chips % (fast * 2) == 0 and (fast * 2) ** 2 <= chips:
        fast *= 2
    return chips // fast, fast, core


def gather_kernel(count, right_in, single_in, right_out, single_out, send_sem, recv_sem):
    slow, fast, core = digits(count)
    me = lax.axis_index("row")
    my_core = lax.rem(me, core)
    chip = lax.div(me, core)
    my_fast = lax.rem(chip, fast)
    my_slow = lax.div(chip, fast)

    def place(a, b, c):
        return (a * fast + b) * core + c

    slow_digits = [lax.rem(my_slow + k, slow) for k in range(slow)]
    fast_digits = [lax.rem(my_fast + k, fast) for k in range(fast)]
    other_core = lax.rem(my_core + 1, core)
    slow_peers = [place(a, my_fast, my_core) for a in slow_digits[1:]]
    fast_peers = [place(my_slow, b, my_core) for b in fast_digits[1:]]
    core_peers = [place(my_slow, my_fast, other_core)] if core == 2 else []
    peers = slow_peers + fast_peers + core_peers

    barrier = pltpu.get_barrier_semaphore()
    for peer in peers:
        pl.semaphore_signal(
            barrier, inc=1, device_id={"row": peer}, device_id_type=pl.DeviceIdType.MESH
        )
    right_out[:, me] = right_in[...]
    single_out[me] = single_in[...]
    pl.semaphore_wait(barrier, len(peers))

    started = []

    def copies(origin, peer, sent, own):
        pair = []
        for which, (entry, result) in enumerate(
            (
                (right_in, right_out.at[:, origin]),
                (single_in, single_out.at[origin]),
            )
        ):
            pair.append(
                pltpu.make_async_remote_copy(
                    src_ref=entry if own else result,
                    dst_ref=result,
                    send_sem=send_sem.at[which, sent],
                    recv_sem=recv_sem.at[which, origin],
                    device_id={"row": peer},
                    device_id_type=pl.DeviceIdType.MESH,
                )
            )
        return pair

    def send(origin, targets, own=False):
        for peer in targets:
            for copy in copies(origin, peer, len(started) // 2, own):
                copy.start()
                started.append(copy)

    def arrive(origin):
        for copy in copies(origin, peers[0], 0, False):
            copy.wait_recv()

    send(me, peers, own=True)
    for a in slow_digits[1:]:
        origin = place(a, my_fast, my_core)
        arrive(origin)
        send(origin, fast_peers + core_peers)
    for b in fast_digits[1:]:
        for a in slow_digits:
            origin = place(a, b, my_core)
            arrive(origin)
            send(origin, core_peers)
    if core == 2:
        for b in fast_digits:
            for a in slow_digits:
                arrive(place(a, b, other_core))
    for copy in started:
        copy.wait_send()


def gather(count, right, single):
    slow, fast, core = digits(count)
    sends = (slow - 1) + slow * (fast - 1) + (slow * fast if core == 2 else 0)
    depth, tokens_here, entries = right.shape
    return pl.pallas_call(
        functools.partial(gather_kernel, count),
        out_shape=(
            jax.ShapeDtypeStruct((depth, count, tokens_here, entries), right.dtype),
            jax.ShapeDtypeStruct((count,) + single.shape, single.dtype),
        ),
        in_specs=[pl.BlockSpec(memory_space=pltpu.VMEM)] * 2,
        out_specs=(pl.BlockSpec(memory_space=pltpu.VMEM),) * 2,
        scratch_shapes=[
            pltpu.SemaphoreType.DMA((2, sends)),
            pltpu.SemaphoreType.DMA((2, count)),
        ],
        compiler_params=pltpu.CompilerParams(
            collective_id=0, has_side_effects=True, vmem_limit_bytes=48 * 2**20
        ),
        name="gather",
    )(right, single)


def dot(a, b):
    return jnp.dot(a, b, preferred_element_type=F32)


def dot_nt(a, b):
    return lax.dot_general(a, b, (((1,), (1,)), ((), ())), preferred_element_type=F32)


def finish_kernel(
    left,
    right,
    counts,
    edge,
    contraction,
    offset,
    ff_scale,
    switch,
    widening,
    narrowing,
    logit_scale,
    edge_logit,
    residue,
    normed_mine,
    normed_all,
    flags,
    asking,
    lookup,
    content,
    gate_matrix,
    merge,
    pair_out,
    single_out,
    total,
    bias,
):
    rows, tokens, width = edge.shape
    entries = right.shape[2]
    pairs = contraction.shape[0]
    heads = edge_logit.shape[0]
    single_width = residue.shape[1]
    head_size = single_width // heads

    total[...] = jnp.zeros_like(total)

    def contract(k, carry):
        mixed = dot(left[...], contraction[k]).astype(BF16)
        columns = []
        for i in range(rows):
            part = mixed[i * entries : (i + 1) * entries]
            columns.append(jnp.concatenate([part[:, :width], part[:, width:]], axis=0))
        panel = jnp.concatenate([right[2 * k], right[2 * k + 1]], axis=1)
        total[...] += dot(panel, jnp.concatenate(columns, axis=1))
        return carry

    lax.fori_loop(0, pairs, contract, 0, unroll=2)

    def transition(i):
        divisor = 1.0 / jnp.maximum(counts[:, i : i + 1], 1.0)
        pair_one = (
            edge[i].astype(F32) + (total[:, i * width : (i + 1) * width] * divisor + offset[...])
        ).astype(BF16)
        normed = standardize_features(pair_one, ff_scale[...]).astype(BF16)
        gated = dot(normed, switch[...])
        lifted = dot(normed, widening[...])
        hidden = (gated / (1.0 + jnp.exp(-gated)) * lifted).astype(BF16)
        pair_two = (pair_one.astype(F32) + dot(hidden, narrowing[...])).astype(BF16)
        pair_out[i] = pair_two
        bias_normed = standardize_features(pair_two, logit_scale[...]).astype(BF16)
        bias[i] = dot_nt(edge_logit[...], bias_normed)

    for i in range(rows):
        transition(i)

    keys = dot(normed_all[...], lookup[...]).astype(BF16)
    values = dot(normed_all[...], content[...]).astype(BF16)
    query = dot(normed_mine[...], asking[...]).astype(BF16).astype(F32)
    gate = jax.nn.sigmoid(dot(normed_mine[...], gate_matrix[...]))
    first = lax.broadcasted_iota(jnp.int32, (heads, single_width), 0) * head_size
    channel = lax.broadcasted_iota(jnp.int32, (heads, single_width), 1)
    mine = ((channel >= first) & (channel < first + head_size)).astype(F32)
    spread = jnp.concatenate([query[i : i + 1] * mine for i in range(rows)], axis=0).astype(BF16)
    scores = dot_nt(spread, keys) * (1.0 / math.sqrt(head_size)) + bias[...].reshape(
        rows * heads, tokens
    )
    live = flags[...] == 1
    scores = jnp.where(live, scores, -1e30)
    peak = jnp.max(scores, axis=-1, keepdims=True)
    expos = jnp.where(live, jnp.exp(scores - peak), 0.0)
    sums = jnp.sum(expos, axis=-1, keepdims=True)
    blended = dot(expos.astype(BF16), values) / sums
    attended = jnp.concatenate(
        [
            jnp.sum(blended[i * heads : (i + 1) * heads] * mine, axis=0, keepdims=True)
            for i in range(rows)
        ],
        axis=0,
    )
    attended = (attended * gate).astype(BF16)
    single_out[...] = (residue[...].astype(F32) + dot(attended, merge[...])).astype(BF16)


def finish(*arrays):
    edge, edge_logit, residue = arrays[3], arrays[11], arrays[12]
    rows, tokens, width = edge.shape
    return pl.pallas_call(
        finish_kernel,
        out_shape=(
            jax.ShapeDtypeStruct(edge.shape, edge.dtype),
            jax.ShapeDtypeStruct(residue.shape, residue.dtype),
        ),
        in_specs=[pl.BlockSpec(memory_space=pltpu.VMEM)] * len(arrays),
        out_specs=(pl.BlockSpec(memory_space=pltpu.VMEM),) * 2,
        scratch_shapes=[
            pltpu.VMEM((tokens, rows * width), F32),
            pltpu.VMEM((rows, edge_logit.shape[0], tokens), F32),
        ],
        compiler_params=pltpu.CompilerParams(vmem_limit_bytes=56 * 2**20),
        name="finish",
    )(*arrays)


def local(
    sequence_features,
    edge_features,
    residue_features,
    polymer_labels,
    polymer_membership,
    present_residue_flags,
    sequence_scaling_vector,
    first_embedding_matrix,
    second_embedding_matrix,
    contraction_matrix,
    contraction_offset,
    feedforward_scaling_vector,
    feedforward_switch_matrix,
    widening_matrix,
    narrowing_matrix,
    logit_scaling_vector,
    edge_logit_matrix,
    residue_scaling_vector,
    asking_matrix,
    lookup_matrix,
    content_matrix,
    heads_sigmoid_matrix,
    heads_merge_matrix,
):
    rows, tokens, width = edge_features.shape
    entries, _, depth = sequence_features.shape
    factors = first_embedding_matrix.shape[1]
    chains = polymer_membership.shape[0]
    single_width = residue_features.shape[1]
    count = lax.axis_size("row")
    first_token = lax.axis_index("row") * rows

    normed_single = standardize_features(residue_features, residue_scaling_vector).astype(BF16)
    onehot_all = (
        polymer_labels[:, None] == jnp.arange(chains, dtype=jnp.int32)[None, :]
    ).astype(F32)
    onehot_mine = lax.dynamic_slice_in_dim(onehot_all, first_token, rows, 0)
    membership = polymer_membership.astype(F32)
    present = jnp.dot(onehot_mine, membership, precision=highest)
    shared = jnp.dot(membership, membership.T, precision=highest)
    counts = jnp.dot(
        jnp.dot(onehot_all, shared, precision=highest), onehot_mine.T, precision=highest
    )

    alignment = standardize_features(
        sequence_features.transpose(1, 0, 2), sequence_scaling_vector
    ).astype(BF16)
    left = (
        lax.dot_general(
            alignment,
            first_embedding_matrix,
            (((2,), (0,)), ((), ())),
            preferred_element_type=F32,
        )
        * present[:, :, None]
    ).astype(BF16)
    right = (
        lax.dot_general(
            second_embedding_matrix,
            alignment,
            (((0,), (2,)), ((), ())),
            preferred_element_type=F32,
        )
        * present[None]
    ).astype(BF16)

    right_all, single_all = gather(count, right, normed_single)
    paired = contraction_matrix.reshape(factors, factors // 2, 2 * width).transpose(1, 0, 2)
    return finish(
        left.reshape(rows * entries, factors),
        right_all.reshape(factors, tokens, entries),
        counts,
        edge_features,
        paired,
        contraction_offset[None],
        feedforward_scaling_vector[None],
        feedforward_switch_matrix,
        widening_matrix,
        narrowing_matrix,
        logit_scaling_vector[None],
        edge_logit_matrix.T,
        residue_features,
        normed_single,
        single_all.reshape(tokens, single_width),
        present_residue_flags[None],
        asking_matrix,
        lookup_matrix,
        content_matrix,
        heads_sigmoid_matrix,
        heads_merge_matrix,
    )


def solution(mesh):
    placed = (
        P("grp", "row", None),
        P(("grp", "row"), None, None),
        P(("grp", "row"), None),
        P("grp"),
        P("grp", None),
        P("grp"),
        P(),
        P(),
        P(),
        P(),
        P(),
        P(),
        P(),
        P(),
        P(),
        P(),
        P(),
        P(),
        P(),
        P(),
        P(),
        P(),
        P(),
    )
    return jax.shard_map(
        local,
        mesh=mesh,
        in_specs=placed,
        out_specs=(P(("grp", "row"), None, None), P(("grp", "row"), None)),
        check_vma=False,
    )
```

```python
import functools
import math

import jax
import jax.numpy as jnp
from jax import lax
from jax.experimental import pallas as pl
from jax.experimental.pallas import tpu as pltpu
from jax.sharding import PartitionSpec as P

epsilon = 1e-05
F32 = jnp.float32
BF16 = jnp.bfloat16


def standardize_features(values, scales):
    values = values.astype(F32)
    centred = values - jnp.mean(values, axis=-1, keepdims=True)
    spread = jnp.mean(centred * centred, axis=-1, keepdims=True)
    return centred * lax.rsqrt(spread + epsilon) * scales


def digits(count):
    core = 2 if count % 2 == 0 else 1
    chips = count // core
    fast = 1
    while chips % (fast * 2) == 0 and (fast * 2) ** 2 <= chips:
        fast *= 2
    return chips // fast, fast, core


def dot(a, b):
    return jnp.dot(a, b, preferred_element_type=F32)


def dot_nt(a, b):
    return lax.dot_general(a, b, (((1,), (1,)), ((), ())), preferred_element_type=F32)


def kernel(
    count,
    alignment,
    edge,
    residue,
    labels_all,
    labels_blocks,
    membership,
    flags,
    alignment_scale,
    first,
    second,
    contraction,
    offset,
    ff_scale,
    switch,
    widening,
    narrowing,
    logit_scale,
    edge_logit,
    residue_scale,
    asking,
    lookup,
    content,
    gate_matrix,
    merge,
    pair_out,
    single_out,
    normed,
    turned,
    mine_block,
    blocks,
    mixed,
    panel,
    bias,
    divisors,
    send_sem,
    recv_sem,
):
    rows, tokens, width = edge.shape
    chains, entries = membership.shape
    factors = first.shape[1]
    heads = edge_logit.shape[0]
    single_width = residue.shape[1]
    head_size = single_width // heads
    chunks = single_width // entries

    slow, fast, core = digits(count)
    me = lax.axis_index("row")
    my_core = lax.rem(me, core)
    chip = lax.div(me, core)
    my_fast = lax.rem(chip, fast)
    my_slow = lax.div(chip, fast)

    def place(a, b, c):
        return (a * fast + b) * core + c

    slow_digits = [lax.rem(my_slow + k, slow) for k in range(slow)]
    fast_digits = [lax.rem(my_fast + k, fast) for k in range(fast)]
    other_core = lax.rem(my_core + 1, core)
    slow_peers = [place(a, my_fast, my_core) for a in slow_digits[1:]]
    fast_peers = [place(my_slow, b, my_core) for b in fast_digits[1:]]
    core_peers = [place(my_slow, my_fast, other_core)] if core == 2 else []
    peers = slow_peers + fast_peers + core_peers

    barrier = pltpu.get_barrier_semaphore()
    for peer in peers:
        pl.semaphore_signal(
            barrier, inc=1, device_id={"row": peer}, device_id_type=pl.DeviceIdType.MESH
        )

    started = []

    def block_copy(origin, peer, sent, own):
        return pltpu.make_async_remote_copy(
            src_ref=mine_block if own else blocks.at[origin],
            dst_ref=blocks.at[origin],
            send_sem=send_sem.at[sent],
            recv_sem=recv_sem.at[origin],
            device_id={"row": peer},
            device_id_type=pl.DeviceIdType.MESH,
        )

    def send(origin, targets, own=False):
        for peer in targets:
            copy = block_copy(origin, peer, len(started), own)
            copy.start()
            started.append(copy)

    def arrive(origin):
        block_copy(origin, peers[0], 0, False).wait_recv()

    normed_single = standardize_features(residue[...], residue_scale[...]).astype(BF16)
    normed[...] = standardize_features(alignment[...], alignment_scale[...])
    member = membership[...].astype(F32)
    chain_ids = lax.broadcasted_iota(jnp.int32, (chains, rows), 0)
    onehot_mine = (chain_ids == labels_blocks[pl.ds(me, 1), :]).astype(F32)
    present = jnp.concatenate(
        [
            jnp.sum(onehot_mine[:, i : i + 1] * member, axis=0, keepdims=True)
            for i in range(rows)
        ],
        axis=0,
    )
    present_columns = present.T
    lefts = []
    for i in range(rows):
        entry = normed[pl.ds(i, entries, stride=rows), :].astype(BF16)
        turned[:, i, :] = dot_nt(second[...], entry) * present[i : i + 1]
        lefts.append((dot(entry, first[...]) * present_columns[:, i : i + 1]).astype(BF16))
    mine_block[:factors] = turned[...].astype(BF16)
    for t in range(chunks):
        mine_block[factors + t] = normed_single[:, t * entries : (t + 1) * entries]

    pl.semaphore_wait(barrier, len(peers))
    send(me, peers, own=True)
    blocks[me] = mine_block[...]

    def mix(start, stop):
        for i in range(rows):
            for k in range(start, stop):
                part = dot(lefts[i], contraction[k]).astype(BF16)
                for u in range(2):
                    top = (2 * k + u) * entries
                    mixed[top : top + entries, i * width : (i + 1) * width] = part[
                        :, u * width : (u + 1) * width
                    ]

    pairs = contraction.shape[0]
    mix(0, pairs // 2)
    for a in slow_digits[1:]:
        origin = place(a, my_fast, my_core)
        arrive(origin)
        send(origin, fast_peers + core_peers)
    mix(pairs // 2, pairs)
    for b in fast_digits[1:]:
        for a in slow_digits:
            origin = place(a, b, my_core)
            arrive(origin)
            send(origin, core_peers)

    query = dot(normed_single, asking[...]).astype(BF16).astype(F32)
    gate = jax.nn.sigmoid(dot(normed_single, gate_matrix[...]))
    onehot_all = (
        lax.broadcasted_iota(jnp.int32, (chains, tokens), 0) == labels_all[...]
    ).astype(F32)
    counts = dot(dot_nt(present, member), onehot_all)
    divisors[...] = (1.0 / jnp.maximum(counts, 1.0)).T

    if core == 2:
        for b in fast_digits:
            for a in slow_digits:
                arrive(place(a, b, other_core))

    def gathered(index):
        return blocks[:, index].astype(F32).reshape(tokens, entries).astype(BF16)

    for d in range(factors):
        panel[:, d * entries : (d + 1) * entries] = gathered(d)
    normed_all = jnp.concatenate([gathered(factors + t) for t in range(chunks)], axis=1)

    step = math.gcd(tokens, 128)
    group = 2 if rows % 2 == 0 else 1
    def finish(j, carry):
        j = pl.multiple_of(j * step, step)
        for i0 in range(0, rows, group):
            update = dot(
                panel[pl.ds(j, step)], mixed[:, i0 * width : (i0 + group) * width]
            )
            for i in range(i0, i0 + group):
                part = update[:, (i - i0) * width : (i - i0 + 1) * width]
                part = part * divisors[pl.ds(j, step), i : i + 1] + offset[...]
                pair_one = (edge[i, pl.ds(j, step)].astype(F32) + part).astype(BF16)
                normed_pair = standardize_features(pair_one, ff_scale[...]).astype(BF16)
                gated = dot(normed_pair, switch[...])
                lifted = dot(normed_pair, widening[...])
                hidden = (gated / (1.0 + jnp.exp(-gated)) * lifted).astype(BF16)
                pair_two = (pair_one.astype(F32) + dot(hidden, narrowing[...])).astype(BF16)
                pair_out[i, pl.ds(j, step)] = pair_two
                bias_normed = standardize_features(pair_two, logit_scale[...]).astype(BF16)
                bias[i, :, pl.ds(j, step)] = dot_nt(edge_logit[...], bias_normed)
        return carry

    lax.fori_loop(0, tokens // step, finish, 0)

    keys = dot(normed_all, lookup[...]).astype(BF16)
    values = dot(normed_all, content[...]).astype(BF16)
    low = lax.broadcasted_iota(jnp.int32, (heads, single_width), 0) * head_size
    channel = lax.broadcasted_iota(jnp.int32, (heads, single_width), 1)
    mine = ((channel >= low) & (channel < low + head_size)).astype(F32)
    spread = jnp.concatenate([query[i : i + 1] * mine for i in range(rows)], axis=0).astype(BF16)
    scores = dot_nt(spread, keys) * (1.0 / math.sqrt(head_size)) + bias[...].reshape(
        rows * heads, tokens
    )
    live = flags[...] == 1
    scores = jnp.where(live, scores, -1e30)
    peak = jnp.max(scores, axis=-1, keepdims=True)
    expos = jnp.where(live, jnp.exp(scores - peak), 0.0)
    sums = jnp.sum(expos, axis=-1, keepdims=True)
    blended = dot(expos.astype(BF16), values) / sums
    attended = jnp.concatenate(
        [
            jnp.sum(blended[i * heads : (i + 1) * heads] * mine, axis=0, keepdims=True)
            for i in range(rows)
        ],
        axis=0,
    )
    attended = (attended * gate).astype(BF16)
    single_out[...] = (residue[...].astype(F32) + dot(attended, merge[...])).astype(BF16)
    for copy in started:
        copy.wait_send()


def local(
    sequence_features,
    edge_features,
    residue_features,
    polymer_labels,
    polymer_membership,
    present_residue_flags,
    sequence_scaling_vector,
    first_embedding_matrix,
    second_embedding_matrix,
    contraction_matrix,
    contraction_offset,
    feedforward_scaling_vector,
    feedforward_switch_matrix,
    widening_matrix,
    narrowing_matrix,
    logit_scaling_vector,
    edge_logit_matrix,
    residue_scaling_vector,
    asking_matrix,
    lookup_matrix,
    content_matrix,
    heads_sigmoid_matrix,
    heads_merge_matrix,
):
    entries, rows, depth = sequence_features.shape
    tokens, width = edge_features.shape[1:]
    factors = first_embedding_matrix.shape[1]
    heads = edge_logit_matrix.shape[1]
    count = lax.axis_size("row")
    slow, fast, core = digits(count)
    sends = (slow - 1) + slow * (fast - 1) + (slow * fast if core == 2 else 0)
    layers = factors + residue_features.shape[1] // entries
    arrays = (
        sequence_features.reshape(entries * rows, depth),
        edge_features,
        residue_features,
        polymer_labels[None],
        polymer_labels.reshape(count, rows),
        polymer_membership,
        present_residue_flags[None],
        sequence_scaling_vector[None],
        first_embedding_matrix,
        second_embedding_matrix.T,
        contraction_matrix.reshape(factors, factors // 2, 2 * width).transpose(1, 0, 2),
        contraction_offset[None],
        feedforward_scaling_vector[None],
        feedforward_switch_matrix,
        widening_matrix,
        narrowing_matrix,
        logit_scaling_vector[None],
        edge_logit_matrix.T,
        residue_scaling_vector[None],
        asking_matrix,
        lookup_matrix,
        content_matrix,
        heads_sigmoid_matrix,
        heads_merge_matrix,
    )
    return pl.pallas_call(
        functools.partial(kernel, count),
        out_shape=(
            jax.ShapeDtypeStruct(edge_features.shape, edge_features.dtype),
            jax.ShapeDtypeStruct(residue_features.shape, residue_features.dtype),
        ),
        in_specs=[pl.BlockSpec(memory_space=pltpu.VMEM)] * len(arrays),
        out_specs=(pl.BlockSpec(memory_space=pltpu.VMEM),) * 2,
        scratch_shapes=[
            pltpu.VMEM((entries * rows, depth), F32),
            pltpu.VMEM((factors, rows, entries), F32),
            pltpu.VMEM((layers, rows, entries), BF16),
            pltpu.VMEM((count, layers, rows, entries), BF16),
            pltpu.VMEM((factors * entries, rows * width), BF16),
            pltpu.VMEM((tokens, factors * entries), BF16),
            pltpu.VMEM((rows, heads, tokens), F32),
            pltpu.VMEM((tokens, rows), F32),
            pltpu.SemaphoreType.DMA((sends,)),
            pltpu.SemaphoreType.DMA((count,)),
        ],
        compiler_params=pltpu.CompilerParams(
            collective_id=0, has_side_effects=True, vmem_limit_bytes=56 * 2**20
        ),
        name="trunk",
    )(*arrays)


def solution(mesh):
    placed = (
        P("grp", "row", None),
        P(("grp", "row"), None, None),
        P(("grp", "row"), None),
        P("grp"),
        P("grp", None),
        P("grp"),
        P(),
        P(),
        P(),
        P(),
        P(),
        P(),
        P(),
        P(),
        P(),
        P(),
        P(),
        P(),
        P(),
        P(),
        P(),
        P(),
        P(),
    )
    return jax.shard_map(
        local,
        mesh=mesh,
        in_specs=placed,
        out_specs=(P(("grp", "row"), None, None), P(("grp", "row"), None)),
        check_vma=False,
    )
```

```python
import functools
import math

import jax
import jax.numpy as jnp
from jax import lax
from jax.experimental import pallas as pl
from jax.experimental.pallas import tpu as pltpu
from jax.sharding import PartitionSpec as P

epsilon = 1e-05
F32 = jnp.float32
BF16 = jnp.bfloat16


def standardize_features(values, scales):
    values = values.astype(F32)
    centred = values - jnp.mean(values, axis=-1, keepdims=True)
    spread = jnp.mean(centred * centred, axis=-1, keepdims=True)
    return centred * lax.rsqrt(spread + epsilon) * scales


def digits(count):
    core = 2 if count % 2 == 0 else 1
    chips = count // core
    fast = 1
    while chips % (fast * 2) == 0 and (fast * 2) ** 2 <= chips:
        fast *= 2
    return chips // fast, fast, core


def dot(a, b):
    return jnp.dot(a, b, preferred_element_type=F32)


def dot_nt(a, b):
    return lax.dot_general(a, b, (((1,), (1,)), ((), ())), preferred_element_type=F32)


def kernel(
    count,
    alignment,
    edge_hbm,
    residue,
    labels_all,
    membership,
    flags,
    alignment_scale,
    first,
    second,
    contraction_hbm,
    offset,
    ff_scale,
    switch_hbm,
    widening_hbm,
    narrowing_hbm,
    logit_scale,
    edge_logit,
    residue_scale,
    asking_hbm,
    lookup_hbm,
    content_hbm,
    gate_matrix_hbm,
    merge_hbm,
    pair_out,
    single_out,
    turned,
    left,
    spread_matrix,
    edge,
    contraction,
    switch,
    widening,
    narrowing,
    asking,
    lookup,
    content,
    gate_matrix,
    merge,
    mine_block,
    blocks,
    mixed,
    panel,
    bias,
    divisors,
    send_sem,
    recv_sem,
    load_sem,
):
    rows, tokens, width = edge_hbm.shape
    chains, entries = membership.shape
    factors = first.shape[0]
    heads = edge_logit.shape[0]
    single_width = residue.shape[1]
    head_size = single_width // heads
    chunks = single_width // entries

    loads = [
        pltpu.make_async_copy(source, target, load_sem.at[index])
        for index, (source, target) in enumerate(
            (
                (contraction_hbm, contraction),
                (asking_hbm, asking),
                (gate_matrix_hbm, gate_matrix),
                (edge_hbm, edge),
                (switch_hbm, switch),
                (widening_hbm, widening),
                (narrowing_hbm, narrowing),
                (lookup_hbm, lookup),
                (content_hbm, content),
                (merge_hbm, merge),
            )
        )
    ]
    for load in loads:
        load.start()

    slow, fast, core = digits(count)
    me = lax.axis_index("row")
    my_core = lax.rem(me, core)
    chip = lax.div(me, core)
    my_fast = lax.rem(chip, fast)
    my_slow = lax.div(chip, fast)

    def place(a, b, c):
        return (a * fast + b) * core + c

    slow_digits = [lax.rem(my_slow + k, slow) for k in range(slow)]
    fast_digits = [lax.rem(my_fast + k, fast) for k in range(fast)]
    other_core = lax.rem(my_core + 1, core)
    slow_peers = [place(a, my_fast, my_core) for a in slow_digits[1:]]
    fast_peers = [place(my_slow, b, my_core) for b in fast_digits[1:]]
    core_peers = [place(my_slow, my_fast, other_core)] if core == 2 else []
    peers = slow_peers + fast_peers + core_peers

    barrier = pltpu.get_barrier_semaphore()
    for peer in peers:
        pl.semaphore_signal(
            barrier, inc=1, device_id={"row": peer}, device_id_type=pl.DeviceIdType.MESH
        )

    started = []

    def block_copy(origin, peer, sent, own):
        return pltpu.make_async_remote_copy(
            src_ref=mine_block if own else blocks.at[origin],
            dst_ref=blocks.at[origin],
            send_sem=send_sem.at[sent],
            recv_sem=recv_sem.at[origin],
            device_id={"row": peer},
            device_id_type=pl.DeviceIdType.MESH,
        )

    def send(origin, targets, own=False):
        for peer in targets:
            copy = block_copy(origin, peer, len(started), own)
            copy.start()
            started.append(copy)

    def arrive(origin):
        block_copy(origin, peers[0], 0, False).wait_recv()

    normed_single = standardize_features(residue[...], residue_scale[...]).astype(BF16)
    member = membership[...].astype(F32)
    onehot_all = (
        lax.broadcasted_iota(jnp.int32, (chains, tokens), 0) == labels_all[...]
    ).astype(F32)
    here = lax.broadcasted_iota(jnp.int32, (tokens, rows), 1) + me * rows
    chosen = (lax.broadcasted_iota(jnp.int32, (tokens, rows), 0) == here).astype(F32)
    onehot_mine = dot(onehot_all, chosen)
    present = jnp.concatenate(
        [
            jnp.sum(onehot_mine[:, i : i + 1] * member, axis=0, keepdims=True)
            for i in range(rows)
        ],
        axis=0,
    )
    depth = first.shape[1]
    diagonal = lax.broadcasted_iota(jnp.int32, (depth, depth), 0) == lax.broadcasted_iota(
        jnp.int32, (depth, depth), 1
    )
    gains = jnp.sum(jnp.where(diagonal, alignment_scale[...], 0.0), axis=1, keepdims=True)
    both = jnp.concatenate([first[...], second[...]], axis=0)
    for i in range(rows):
        entry = alignment[i].astype(F32)
        entry = entry - jnp.mean(entry, axis=0, keepdims=True)
        variance = jnp.mean(entry * entry, axis=0, keepdims=True)
        entry = (entry * lax.rsqrt(variance + epsilon) * gains).astype(BF16)
        embedded = dot(both, entry) * present[i : i + 1]
        turned[:, i, :] = embedded[factors:]
        left[i] = embedded[:factors].T.astype(BF16)
    mine_block[:factors] = turned[...].astype(BF16)
    for t in range(chunks):
        mine_block[factors + t] = normed_single[:, t * entries : (t + 1) * entries]

    pl.semaphore_wait(barrier, len(peers))
    send(me, peers, own=True)
    blocks[me] = mine_block[...]

    loads[0].wait()
    spread_matrix[...] = contraction[...].astype(F32)

    def mix(start, stop):
        for k in range(start, stop):
            panels = jnp.concatenate(
                [
                    spread_matrix[pl.ds(2 * k + u, factors, stride=factors), :]
                    for u in range(2)
                ],
                axis=1,
            ).astype(BF16)
            for i in range(rows):
                part = dot(left[i], panels).astype(BF16)
                for u in range(2):
                    top = (2 * k + u) * entries
                    mixed[top : top + entries, i * width : (i + 1) * width] = part[
                        :, u * width : (u + 1) * width
                    ]

    pairs = factors // 2
    mix(0, pairs // 2)
    for a in slow_digits[1:]:
        origin = place(a, my_fast, my_core)
        arrive(origin)
        send(origin, fast_peers + core_peers)
    mix(pairs // 2, pairs)
    for b in fast_digits[1:]:
        for a in slow_digits:
            origin = place(a, b, my_core)
            arrive(origin)
            send(origin, core_peers)

    loads[1].wait()
    loads[2].wait()
    query = dot(normed_single, asking[...]).astype(BF16).astype(F32)
    gate = jax.nn.sigmoid(dot(normed_single, gate_matrix[...]))
    counts = dot(dot_nt(present, member), onehot_all)
    divisors[...] = (1.0 / jnp.maximum(counts, 1.0)).T

    if core == 2:
        for b in fast_digits:
            for a in slow_digits:
                arrive(place(a, b, other_core))

    def gathered(index):
        return blocks[:, index].astype(F32).reshape(tokens, entries).astype(BF16)

    for d in range(factors):
        panel[:, d * entries : (d + 1) * entries] = gathered(d)
    normed_all = jnp.concatenate([gathered(factors + t) for t in range(chunks)], axis=1)

    for load in loads[3:]:
        load.wait()
    step = math.gcd(tokens, 128)
    group = 2 if rows % 2 == 0 else 1
    def finish(j, carry):
        j = pl.multiple_of(j * step, step)
        for i0 in range(0, rows, group):
            update = dot(
                panel[pl.ds(j, step)], mixed[:, i0 * width : (i0 + group) * width]
            )
            for i in range(i0, i0 + group):
                part = update[:, (i - i0) * width : (i - i0 + 1) * width]
                part = part * divisors[pl.ds(j, step), i : i + 1] + offset[...]
                pair_one = (edge[i, pl.ds(j, step)].astype(F32) + part).astype(BF16)
                normed_pair = standardize_features(pair_one, ff_scale[...]).astype(BF16)
                gated = dot(normed_pair, switch[...])
                lifted = dot(normed_pair, widening[...])
                hidden = (gated / (1.0 + jnp.exp(-gated)) * lifted).astype(BF16)
                pair_two = (pair_one.astype(F32) + dot(hidden, narrowing[...])).astype(BF16)
                pair_out[i, pl.ds(j, step)] = pair_two
                bias_normed = standardize_features(pair_two, logit_scale[...]).astype(BF16)
                bias[i, :, pl.ds(j, step)] = dot_nt(edge_logit[...], bias_normed)
        return carry

    lax.fori_loop(0, tokens // step, finish, 0)

    keys = dot(normed_all, lookup[...]).astype(BF16)
    values = dot(normed_all, content[...]).astype(BF16)
    low = lax.broadcasted_iota(jnp.int32, (heads, single_width), 0) * head_size
    channel = lax.broadcasted_iota(jnp.int32, (heads, single_width), 1)
    mine = ((channel >= low) & (channel < low + head_size)).astype(F32)
    spread = jnp.concatenate([query[i : i + 1] * mine for i in range(rows)], axis=0).astype(BF16)
    scores = dot_nt(spread, keys) * (1.0 / math.sqrt(head_size)) + bias[...].reshape(
        rows * heads, tokens
    )
    live = flags[...] == 1
    scores = jnp.where(live, scores, -1e30)
    peak = jnp.max(scores, axis=-1, keepdims=True)
    expos = jnp.where(live, jnp.exp(scores - peak), 0.0)
    sums = jnp.sum(expos, axis=-1, keepdims=True)
    blended = dot(expos.astype(BF16), values) / sums
    attended = jnp.concatenate(
        [
            jnp.sum(blended[i * heads : (i + 1) * heads] * mine, axis=0, keepdims=True)
            for i in range(rows)
        ],
        axis=0,
    )
    attended = (attended * gate).astype(BF16)
    single_out[...] = (residue[...].astype(F32) + dot(attended, merge[...])).astype(BF16)
    for copy in started:
        copy.wait_send()


def local(
    sequence_features,
    edge_features,
    residue_features,
    polymer_labels,
    polymer_membership,
    present_residue_flags,
    sequence_scaling_vector,
    first_embedding_matrix,
    second_embedding_matrix,
    contraction_matrix,
    contraction_offset,
    feedforward_scaling_vector,
    feedforward_switch_matrix,
    widening_matrix,
    narrowing_matrix,
    logit_scaling_vector,
    edge_logit_matrix,
    residue_scaling_vector,
    asking_matrix,
    lookup_matrix,
    content_matrix,
    heads_sigmoid_matrix,
    heads_merge_matrix,
):
    entries, rows, _ = sequence_features.shape
    tokens, width = edge_features.shape[1:]
    factors = first_embedding_matrix.shape[1]
    heads = edge_logit_matrix.shape[1]
    count = lax.axis_size("row")
    slow, fast, core = digits(count)
    sends = (slow - 1) + slow * (fast - 1) + (slow * fast if core == 2 else 0)
    layers = factors + residue_features.shape[1] // entries
    arrays = (
        sequence_features.transpose(1, 2, 0),
        edge_features,
        residue_features,
        polymer_labels[None],
        polymer_membership,
        present_residue_flags[None],
        sequence_scaling_vector[None],
        first_embedding_matrix.T,
        second_embedding_matrix.T,
        contraction_matrix,
        contraction_offset[None],
        feedforward_scaling_vector[None],
        feedforward_switch_matrix,
        widening_matrix,
        narrowing_matrix,
        logit_scaling_vector[None],
        edge_logit_matrix.T,
        residue_scaling_vector,
        asking_matrix,
        lookup_matrix,
        content_matrix,
        heads_sigmoid_matrix,
        heads_merge_matrix,
    )
    large = (1, 9, 12, 13, 14, 18, 19, 20, 21, 22)
    return pl.pallas_call(
        functools.partial(kernel, count),
        out_shape=(
            jax.ShapeDtypeStruct(edge_features.shape, edge_features.dtype),
            jax.ShapeDtypeStruct(residue_features.shape, residue_features.dtype),
        ),
        in_specs=[
            pl.BlockSpec(memory_space=pl.ANY if index in large else pltpu.VMEM)
            for index in range(len(arrays))
        ],
        out_specs=(pl.BlockSpec(memory_space=pltpu.VMEM),) * 2,
        scratch_shapes=[
            pltpu.VMEM((factors, rows, entries), F32),
            pltpu.VMEM((rows, entries, factors), BF16),
            pltpu.VMEM(contraction_matrix.shape, F32),
            pltpu.VMEM(arrays[1].shape, BF16),
            pltpu.VMEM(arrays[9].shape, BF16),
            pltpu.VMEM(arrays[12].shape, BF16),
            pltpu.VMEM(arrays[13].shape, BF16),
            pltpu.VMEM(arrays[14].shape, BF16),
            pltpu.VMEM(arrays[18].shape, BF16),
            pltpu.VMEM(arrays[19].shape, BF16),
            pltpu.VMEM(arrays[20].shape, BF16),
            pltpu.VMEM(arrays[21].shape, BF16),
            pltpu.VMEM(arrays[22].shape, BF16),
            pltpu.VMEM((layers, rows, entries), BF16),
            pltpu.VMEM((count, layers, rows, entries), BF16),
            pltpu.VMEM((factors * entries, rows * width), BF16),
            pltpu.VMEM((tokens, factors * entries), BF16),
            pltpu.VMEM((rows, heads, tokens), F32),
            pltpu.VMEM((tokens, rows), F32),
            pltpu.SemaphoreType.DMA((sends,)),
            pltpu.SemaphoreType.DMA((count,)),
            pltpu.SemaphoreType.DMA((len(large),)),
        ],
        compiler_params=pltpu.CompilerParams(
            collective_id=0, has_side_effects=True, vmem_limit_bytes=44 * 2**20
        ),
        name="trunk",
    )(*arrays)


def solution(mesh):
    placed = (
        P("grp", "row", None),
        P(("grp", "row"), None, None),
        P(("grp", "row"), None),
        P("grp"),
        P("grp", None),
        P("grp"),
        P(),
        P(),
        P(),
        P(),
        P(),
        P(),
        P(),
        P(),
        P(),
        P(),
        P(),
        P(),
        P(),
        P(),
        P(),
        P(),
        P(),
    )
    return jax.shard_map(
        local,
        mesh=mesh,
        in_specs=placed,
        out_specs=(P(("grp", "row"), None, None), P(("grp", "row"), None)),
        check_vma=False,
    )
```

```python
import functools
import math

import jax
import jax.numpy as jnp
from jax import lax
from jax.experimental import pallas as pl
from jax.experimental.pallas import tpu as pltpu
from jax.sharding import PartitionSpec as P

epsilon = 1e-05
F32 = jnp.float32
BF16 = jnp.bfloat16


def standardize_features(values, scales):
    values = values.astype(F32)
    centred = values - jnp.mean(values, axis=-1, keepdims=True)
    spread = jnp.mean(centred * centred, axis=-1, keepdims=True)
    return centred * lax.rsqrt(spread + epsilon) * scales


def digits(count):
    core = 2 if count % 2 == 0 else 1
    chips = count // core
    fast = 1
    while chips % (fast * 2) == 0 and (fast * 2) ** 2 <= chips:
        fast *= 2
    return chips // fast, fast, core


def dot(a, b):
    return jnp.dot(a, b, preferred_element_type=F32)


def dot_nt(a, b):
    return lax.dot_general(a, b, (((1,), (1,)), ((), ())), preferred_element_type=F32)


def kernel(
    count,
    alignment,
    edge_hbm,
    residue,
    labels_all,
    membership,
    flags,
    alignment_scale,
    first,
    second,
    contraction_hbm,
    offset,
    ff_scale,
    switch_hbm,
    widening_hbm,
    narrowing_hbm,
    logit_scale,
    edge_logit,
    residue_scale,
    asking_hbm,
    lookup_hbm,
    content_hbm,
    gate_matrix_hbm,
    merge_hbm,
    pair_out,
    single_out,
    turned,
    left,
    spread_matrix,
    edge,
    contraction,
    switch,
    widening,
    narrowing,
    asking,
    lookup,
    content,
    gate_matrix,
    merge,
    mine_block,
    blocks,
    mixed,
    panel,
    bias,
    divisors,
    send_sem,
    recv_sem,
    load_sem,
):
    rows, tokens, width = edge_hbm.shape
    chains, entries = membership.shape
    factors = first.shape[0]
    heads = edge_logit.shape[0]
    single_width = residue.shape[1]
    head_size = single_width // heads
    chunks = single_width // entries

    loads = [
        pltpu.make_async_copy(source, target, load_sem.at[index])
        for index, (source, target) in enumerate(
            (
                (contraction_hbm, contraction),
                (asking_hbm, asking),
                (gate_matrix_hbm, gate_matrix),
                (edge_hbm, edge),
                (switch_hbm, switch),
                (widening_hbm, widening),
                (narrowing_hbm, narrowing),
                (lookup_hbm, lookup),
                (content_hbm, content),
                (merge_hbm, merge),
            )
        )
    ]
    for load in loads:
        load.start()

    slow, fast, core = digits(count)
    me = lax.axis_index("row")
    my_core = lax.rem(me, core)
    chip = lax.div(me, core)
    my_fast = lax.rem(chip, fast)
    my_slow = lax.div(chip, fast)

    def place(a, b, c):
        return (a * fast + b) * core + c

    slow_digits = [lax.rem(my_slow + k, slow) for k in range(slow)]
    fast_digits = [lax.rem(my_fast + k, fast) for k in range(fast)]
    other_core = lax.rem(my_core + 1, core)
    slow_peers = [place(a, my_fast, my_core) for a in slow_digits[1:]]
    fast_peers = [place(my_slow, b, my_core) for b in fast_digits[1:]]
    core_peers = [place(my_slow, my_fast, other_core)] if core == 2 else []
    peers = slow_peers + fast_peers + core_peers

    barrier = pltpu.get_barrier_semaphore()
    for peer in peers:
        pl.semaphore_signal(
            barrier, inc=1, device_id={"row": peer}, device_id_type=pl.DeviceIdType.MESH
        )

    started = []

    def block_copy(origin, peer, sent, own):
        return pltpu.make_async_remote_copy(
            src_ref=mine_block if own else blocks.at[origin],
            dst_ref=blocks.at[origin],
            send_sem=send_sem.at[sent],
            recv_sem=recv_sem.at[origin],
            device_id={"row": peer},
            device_id_type=pl.DeviceIdType.MESH,
        )

    def send(origin, targets, own=False):
        for peer in targets:
            copy = block_copy(origin, peer, len(started), own)
            copy.start()
            started.append(copy)

    def arrive(origin):
        block_copy(origin, peers[0], 0, False).wait_recv()

    normed_single = standardize_features(residue[...], residue_scale[...]).astype(BF16)
    member = membership[...].astype(F32)
    onehot_all = (
        lax.broadcasted_iota(jnp.int32, (chains, tokens), 0) == labels_all[...]
    ).astype(F32)
    here = lax.broadcasted_iota(jnp.int32, (tokens, rows), 1) + me * rows
    chosen = (lax.broadcasted_iota(jnp.int32, (tokens, rows), 0) == here).astype(F32)
    onehot_mine = dot(onehot_all, chosen)
    present = jnp.concatenate(
        [
            jnp.sum(onehot_mine[:, i : i + 1] * member, axis=0, keepdims=True)
            for i in range(rows)
        ],
        axis=0,
    )
    depth = first.shape[1]
    diagonal = lax.broadcasted_iota(jnp.int32, (depth, depth), 0) == lax.broadcasted_iota(
        jnp.int32, (depth, depth), 1
    )
    gains = jnp.sum(jnp.where(diagonal, alignment_scale[...], 0.0), axis=1, keepdims=True)
    both = jnp.concatenate([first[...], second[...]], axis=0)
    for i in range(rows):
        entry = alignment[i].astype(F32)
        entry = entry - jnp.mean(entry, axis=0, keepdims=True)
        variance = jnp.mean(entry * entry, axis=0, keepdims=True)
        entry = (entry * lax.rsqrt(variance + epsilon) * gains).astype(BF16)
        embedded = dot(both, entry) * present[i : i + 1]
        turned[:, i, :] = embedded[factors:]
        left[i] = embedded[:factors].T.astype(BF16)
    mine_block[:factors] = turned[...].astype(BF16)
    for t in range(chunks):
        mine_block[factors + t] = normed_single[:, t * entries : (t + 1) * entries]

    pl.semaphore_wait(barrier, len(peers))
    send(me, peers, own=True)
    blocks[me] = mine_block[...]

    loads[0].wait()
    spread_matrix[...] = contraction[...].astype(F32)

    def mix(start, stop):
        for k in range(start, stop):
            panels = jnp.concatenate(
                [
                    spread_matrix[pl.ds(2 * k + u, factors, stride=factors), :]
                    for u in range(2)
                ],
                axis=1,
            ).astype(BF16)
            for i in range(rows):
                part = dot(left[i], panels).astype(BF16)
                for u in range(2):
                    top = (2 * k + u) * entries
                    mixed[top : top + entries, i * width : (i + 1) * width] = part[
                        :, u * width : (u + 1) * width
                    ]

    pairs = factors // 2
    mix(0, pairs // 2)
    for a in slow_digits[1:]:
        origin = place(a, my_fast, my_core)
        arrive(origin)
        send(origin, fast_peers + core_peers)
    mix(pairs // 2, pairs)
    for b in fast_digits[1:]:
        for a in slow_digits:
            origin = place(a, b, my_core)
            arrive(origin)
            send(origin, core_peers)

    loads[1].wait()
    loads[2].wait()
    query = dot(normed_single, asking[...]).astype(BF16).astype(F32)
    gate = jax.nn.sigmoid(dot(normed_single, gate_matrix[...]))
    counts = dot(dot_nt(present, member), onehot_all)
    divisors[...] = (1.0 / jnp.maximum(counts, 1.0)).T

    if core == 2:
        for b in fast_digits:
            for a in slow_digits:
                arrive(place(a, b, other_core))

    def gathered(index):
        return blocks[:, index].astype(F32).reshape(tokens, entries).astype(BF16)

    for d in range(factors):
        panel[:, d * entries : (d + 1) * entries] = gathered(d)
    normed_all = jnp.concatenate([gathered(factors + t) for t in range(chunks)], axis=1)

    for load in loads[3:]:
        load.wait()
    step = math.gcd(tokens, 128)
    group = 2 if rows % 2 == 0 else 1
    def finish(j, carry):
        j = pl.multiple_of(j * step, step)
        for i0 in range(0, rows, group):
            update = dot(
                panel[pl.ds(j, step)], mixed[:, i0 * width : (i0 + group) * width]
            )
            for i in range(i0, i0 + group):
                part = update[:, (i - i0) * width : (i - i0 + 1) * width]
                part = part * divisors[pl.ds(j, step), i : i + 1] + offset[...]
                pair_one = (edge[i, pl.ds(j, step)].astype(F32) + part).astype(BF16)
                normed_pair = standardize_features(pair_one, ff_scale[...]).astype(BF16)
                gated = dot(normed_pair, switch[...])
                lifted = dot(normed_pair, widening[...])
                hidden = (gated / (1.0 + jnp.exp(-gated)) * lifted).astype(BF16)
                pair_two = (pair_one.astype(F32) + dot(hidden, narrowing[...])).astype(BF16)
                pair_out[i, pl.ds(j, step)] = pair_two
                bias_normed = standardize_features(pair_two, logit_scale[...]).astype(BF16)
                bias[i, :, pl.ds(j, step)] = dot_nt(edge_logit[...], bias_normed)
        return carry

    lax.fori_loop(0, tokens // step, finish, 0)

    keys = dot(normed_all, lookup[...]).astype(BF16)
    values = dot(normed_all, content[...]).astype(BF16)
    low = lax.broadcasted_iota(jnp.int32, (heads, single_width), 0) * head_size
    channel = lax.broadcasted_iota(jnp.int32, (heads, single_width), 1)
    mine = ((channel >= low) & (channel < low + head_size)).astype(F32)
    spread = jnp.concatenate([query[i : i + 1] * mine for i in range(rows)], axis=0).astype(BF16)
    scores = dot_nt(spread, keys) * (1.0 / math.sqrt(head_size)) + bias[...].reshape(
        rows * heads, tokens
    )
    live = flags[...] == 1
    scores = jnp.where(live, scores, -1e30)
    peak = jnp.max(scores, axis=-1, keepdims=True)
    expos = jnp.where(live, jnp.exp(scores - peak), 0.0)
    sums = jnp.sum(expos, axis=-1, keepdims=True)
    blended = dot(expos.astype(BF16), values) / sums
    attended = jnp.concatenate(
        [
            jnp.sum(blended[i * heads : (i + 1) * heads] * mine, axis=0, keepdims=True)
            for i in range(rows)
        ],
        axis=0,
    )
    attended = (attended * gate).astype(BF16)
    single_out[...] = (residue[...].astype(F32) + dot(attended, merge[...])).astype(BF16)
    for copy in started:
        copy.wait_send()


def local(
    sequence_features,
    edge_features,
    residue_features,
    polymer_labels,
    polymer_membership,
    present_residue_flags,
    sequence_scaling_vector,
    first_embedding_matrix,
    second_embedding_matrix,
    contraction_matrix,
    contraction_offset,
    feedforward_scaling_vector,
    feedforward_switch_matrix,
    widening_matrix,
    narrowing_matrix,
    logit_scaling_vector,
    edge_logit_matrix,
    residue_scaling_vector,
    asking_matrix,
    lookup_matrix,
    content_matrix,
    heads_sigmoid_matrix,
    heads_merge_matrix,
):
    entries, rows, _ = sequence_features.shape
    tokens, width = edge_features.shape[1:]
    factors = first_embedding_matrix.shape[1]
    heads = edge_logit_matrix.shape[1]
    count = lax.axis_size("row")
    slow, fast, core = digits(count)
    sends = (slow - 1) + slow * (fast - 1) + (slow * fast if core == 2 else 0)
    layers = factors + residue_features.shape[1] // entries
    arrays = (
        sequence_features.transpose(1, 2, 0),
        edge_features,
        residue_features,
        polymer_labels[None],
        polymer_membership,
        present_residue_flags[None],
        sequence_scaling_vector[None],
        first_embedding_matrix.T,
        second_embedding_matrix.T,
        contraction_matrix,
        contraction_offset[None],
        feedforward_scaling_vector[None],
        feedforward_switch_matrix,
        widening_matrix,
        narrowing_matrix,
        logit_scaling_vector[None],
        edge_logit_matrix.T,
        residue_scaling_vector,
        asking_matrix,
        lookup_matrix,
        content_matrix,
        heads_sigmoid_matrix,
        heads_merge_matrix,
    )
    large = (1, 9, 12, 13, 14, 18, 19, 20, 21, 22)
    return pl.pallas_call(
        functools.partial(kernel, count),
        out_shape=(
            jax.ShapeDtypeStruct(edge_features.shape, edge_features.dtype),
            jax.ShapeDtypeStruct(residue_features.shape, residue_features.dtype),
        ),
        in_specs=[
            pl.BlockSpec(memory_space=pl.ANY if index in large else pltpu.VMEM)
            for index in range(len(arrays))
        ],
        out_specs=(pl.BlockSpec(memory_space=pltpu.VMEM),) * 2,
        scratch_shapes=[
            pltpu.VMEM((factors, rows, entries), F32),
            pltpu.VMEM((rows, entries, factors), BF16),
            pltpu.VMEM(contraction_matrix.shape, F32),
            pltpu.VMEM(arrays[1].shape, BF16),
            pltpu.VMEM(arrays[9].shape, BF16),
            pltpu.VMEM(arrays[12].shape, BF16),
            pltpu.VMEM(arrays[13].shape, BF16),
            pltpu.VMEM(arrays[14].shape, BF16),
            pltpu.VMEM(arrays[18].shape, BF16),
            pltpu.VMEM(arrays[19].shape, BF16),
            pltpu.VMEM(arrays[20].shape, BF16),
            pltpu.VMEM(arrays[21].shape, BF16),
            pltpu.VMEM(arrays[22].shape, BF16),
            pltpu.VMEM((layers, rows, entries), BF16),
            pltpu.VMEM((count, layers, rows, entries), BF16),
            pltpu.VMEM((factors * entries, rows * width), BF16),
            pltpu.VMEM((tokens, factors * entries), BF16),
            pltpu.VMEM((rows, heads, tokens), F32),
            pltpu.VMEM((tokens, rows), F32),
            pltpu.SemaphoreType.DMA((sends,)),
            pltpu.SemaphoreType.DMA((count,)),
            pltpu.SemaphoreType.DMA((len(large),)),
        ],
        compiler_params=pltpu.CompilerParams(
            collective_id=0, has_side_effects=True, vmem_limit_bytes=56 * 2**20
        ),
        name="trunk",
    )(*arrays)


def solution(mesh):
    placed = (
        P("grp", "row", None),
        P(("grp", "row"), None, None),
        P(("grp", "row"), None),
        P("grp"),
        P("grp", None),
        P("grp"),
        P(),
        P(),
        P(),
        P(),
        P(),
        P(),
        P(),
        P(),
        P(),
        P(),
        P(),
        P(),
        P(),
        P(),
        P(),
        P(),
        P(),
    )
    return jax.shard_map(
        local,
        mesh=mesh,
        in_specs=placed,
        out_specs=(P(("grp", "row"), None, None), P(("grp", "row"), None)),
        check_vma=False,
    )
```

```python
import functools
import math

import jax
import jax.numpy as jnp
from jax import lax
from jax.experimental import pallas as pl
from jax.experimental.pallas import tpu as pltpu
from jax.sharding import PartitionSpec as P

epsilon = 1e-05
F32 = jnp.float32
BF16 = jnp.bfloat16


def standardize_features(values, scales):
    values = values.astype(F32)
    centred = values - jnp.mean(values, axis=-1, keepdims=True)
    spread = jnp.mean(centred * centred, axis=-1, keepdims=True)
    return centred * lax.rsqrt(spread + epsilon) * scales


def digits(count):
    core = 2 if count % 2 == 0 else 1
    chips = count // core
    fast = 1
    while chips % (fast * 2) == 0 and (fast * 2) ** 2 <= chips:
        fast *= 2
    return chips // fast, fast, core


def dot(a, b):
    return jnp.dot(a, b, preferred_element_type=F32)


def dot_nt(a, b):
    return lax.dot_general(a, b, (((1,), (1,)), ((), ())), preferred_element_type=F32)


def kernel(
    count,
    alignment,
    edge_hbm,
    residue,
    labels_all,
    membership,
    flags,
    alignment_scale,
    first,
    second,
    contraction_hbm,
    offset,
    ff_scale,
    switch_hbm,
    widening_hbm,
    narrowing_hbm,
    logit_scale,
    edge_logit,
    residue_scale,
    asking_hbm,
    lookup_hbm,
    content_hbm,
    gate_matrix_hbm,
    merge_hbm,
    pair_out,
    single_out,
    turned,
    left,
    spread_matrix,
    edge,
    contraction,
    switch,
    widening,
    narrowing,
    asking,
    lookup,
    content,
    gate_matrix,
    merge,
    mine_block,
    blocks,
    mixed,
    panel,
    bias,
    divisors,
    send_sem,
    recv_sem,
    load_sem,
):
    rows, tokens, width = edge_hbm.shape
    chains, entries = membership.shape
    factors = first.shape[0]
    heads = edge_logit.shape[0]
    single_width = residue.shape[1]
    head_size = single_width // heads
    chunks = single_width // entries
    layers = factors + chunks

    loads = [
        pltpu.make_async_copy(source, target, load_sem.at[index])
        for index, (source, target) in enumerate(
            (
                (contraction_hbm, contraction),
                (asking_hbm, asking),
                (gate_matrix_hbm, gate_matrix),
                (edge_hbm, edge),
                (switch_hbm, switch),
                (widening_hbm, widening),
                (narrowing_hbm, narrowing),
                (lookup_hbm, lookup),
                (content_hbm, content),
                (merge_hbm, merge),
            )
        )
    ]
    for load in loads:
        load.start()

    slow, fast, core = digits(count)
    me = lax.axis_index("row")
    my_core = lax.rem(me, core)
    chip = lax.div(me, core)
    my_fast = lax.rem(chip, fast)
    my_slow = lax.div(chip, fast)

    def place(a, b, c):
        return (a * fast + b) * core + c

    slow_digits = [lax.rem(my_slow + k, slow) for k in range(slow)]
    fast_digits = [lax.rem(my_fast + k, fast) for k in range(fast)]
    other_core = lax.rem(my_core + 1, core)
    slow_peers = [place(a, my_fast, my_core) for a in slow_digits[1:]]
    fast_peers = [place(my_slow, b, my_core) for b in fast_digits[1:]]
    core_peers = [place(my_slow, my_fast, other_core)] if core == 2 else []
    peers = slow_peers + fast_peers + core_peers

    barrier = pltpu.get_barrier_semaphore()
    for peer in peers:
        pl.semaphore_signal(
            barrier, inc=1, device_id={"row": peer}, device_id_type=pl.DeviceIdType.MESH
        )

    started = []

    def block_copy(origin, peer, sent, own):
        return pltpu.make_async_remote_copy(
            src_ref=mine_block if own else blocks.at[origin],
            dst_ref=blocks.at[origin],
            send_sem=send_sem.at[sent],
            recv_sem=recv_sem.at[origin],
            device_id={"row": peer},
            device_id_type=pl.DeviceIdType.MESH,
        )

    def send(origin, targets, own=False):
        for peer in targets:
            copy = block_copy(origin, peer, len(started), own)
            copy.start()
            started.append(copy)

    def arrive(origin):
        block_copy(origin, peers[0], 0, False).wait_recv()

    normed_single = standardize_features(residue[...], residue_scale[...]).astype(BF16)
    member = membership[...].astype(F32)
    onehot_all = (
        lax.broadcasted_iota(jnp.int32, (chains, tokens), 0) == labels_all[...]
    ).astype(F32)
    here = lax.broadcasted_iota(jnp.int32, (tokens, rows), 1) + me * rows
    chosen = (lax.broadcasted_iota(jnp.int32, (tokens, rows), 0) == here).astype(F32)
    onehot_mine = dot(onehot_all, chosen)
    present = jnp.concatenate(
        [
            jnp.sum(onehot_mine[:, i : i + 1] * member, axis=0, keepdims=True)
            for i in range(rows)
        ],
        axis=0,
    )
    depth = first.shape[1]
    diagonal = lax.broadcasted_iota(jnp.int32, (depth, depth), 0) == lax.broadcasted_iota(
        jnp.int32, (depth, depth), 1
    )
    gains = jnp.sum(jnp.where(diagonal, alignment_scale[...], 0.0), axis=1, keepdims=True)
    both = jnp.concatenate([first[...], second[...]], axis=0)
    for i in range(rows):
        entry = alignment[i].astype(F32)
        entry = entry - jnp.mean(entry, axis=0, keepdims=True)
        variance = jnp.mean(entry * entry, axis=0, keepdims=True)
        entry = (entry * lax.rsqrt(variance + epsilon) * gains).astype(BF16)
        embedded = dot(both, entry) * present[i : i + 1]
        turned[:, i, :] = embedded[factors:]
        left[i] = embedded[:factors].T.astype(BF16)
    mine_block[:factors] = turned[...].astype(BF16)
    for t in range(chunks):
        mine_block[factors + t] = normed_single[:, t * entries : (t + 1) * entries]

    pl.semaphore_wait(barrier, len(peers))
    send(me, peers, own=True)
    blocks[me] = mine_block[...]

    loads[0].wait()
    spread_matrix[...] = contraction[...].astype(F32)

    def mix(start, stop):
        for k in range(start, stop):
            panels = jnp.concatenate(
                [
                    spread_matrix[pl.ds(2 * k + u, factors, stride=factors), :]
                    for u in range(2)
                ],
                axis=1,
            ).astype(BF16)
            for i in range(rows):
                part = dot(left[i], panels).astype(BF16)
                for u in range(2):
                    top = (2 * k + u) * entries
                    mixed[top : top + entries, i * width : (i + 1) * width] = part[
                        :, u * width : (u + 1) * width
                    ]

    pairs = factors // 2
    def settle(a, b):
        base = (a * fast + b) * core
        place_rows = pl.ds(pl.multiple_of(base * rows, core * rows), core * rows)
        for d in range(layers):
            layer = blocks[pl.ds(base, core), d].astype(F32)
            panel[place_rows, d * entries : (d + 1) * entries] = layer.reshape(
                core * rows, entries
            ).astype(BF16)

    parts = slow + 1
    bounds = [pairs * k // parts for k in range(parts + 1)]
    mix(bounds[0], bounds[1])
    for k, a in enumerate(slow_digits[1:]):
        origin = place(a, my_fast, my_core)
        arrive(origin)
        send(origin, fast_peers + core_peers)
        mix(bounds[k + 1], bounds[k + 2])
    mix(bounds[slow], bounds[parts])
    for a in slow_digits:
        if core == 2:
            arrive(place(a, my_fast, other_core))
        settle(a, my_fast)

    loads[1].wait()
    loads[2].wait()
    query = dot(normed_single, asking[...]).astype(BF16).astype(F32)
    gate = jax.nn.sigmoid(dot(normed_single, gate_matrix[...]))
    counts = dot(dot_nt(present, member), onehot_all)
    divisors[...] = (1.0 / jnp.maximum(counts, 1.0)).T

    for b in fast_digits[1:]:
        for a in slow_digits:
            origin = place(a, b, my_core)
            arrive(origin)
            send(origin, core_peers)
    for b in fast_digits[1:]:
        for a in slow_digits:
            if core == 2:
                arrive(place(a, b, other_core))
            settle(a, b)
    normed_all = panel[:, factors * entries :]

    for load in loads[3:]:
        load.wait()
    step = math.gcd(tokens, 128)
    group = 2 if rows % 2 == 0 else 1
    def finish(j, carry):
        j = pl.multiple_of(j * step, step)
        for i0 in range(0, rows, group):
            update = dot(
                panel[pl.ds(j, step), : factors * entries], mixed[:, i0 * width : (i0 + group) * width]
            )
            for i in range(i0, i0 + group):
                part = update[:, (i - i0) * width : (i - i0 + 1) * width]
                part = part * divisors[pl.ds(j, step), i : i + 1] + offset[...]
                pair_one = (edge[i, pl.ds(j, step)].astype(F32) + part).astype(BF16)
                normed_pair = standardize_features(pair_one, ff_scale[...]).astype(BF16)
                gated = dot(normed_pair, switch[...])
                lifted = dot(normed_pair, widening[...])
                hidden = (gated / (1.0 + jnp.exp(-gated)) * lifted).astype(BF16)
                pair_two = (pair_one.astype(F32) + dot(hidden, narrowing[...])).astype(BF16)
                pair_out[i, pl.ds(j, step)] = pair_two
                bias_normed = standardize_features(pair_two, logit_scale[...]).astype(BF16)
                bias[i, :, pl.ds(j, step)] = dot_nt(edge_logit[...], bias_normed)
        return carry

    lax.fori_loop(0, tokens // step, finish, 0)

    keys = dot(normed_all, lookup[...]).astype(BF16)
    values = dot(normed_all, content[...]).astype(BF16)
    low = lax.broadcasted_iota(jnp.int32, (heads, single_width), 0) * head_size
    channel = lax.broadcasted_iota(jnp.int32, (heads, single_width), 1)
    mine = ((channel >= low) & (channel < low + head_size)).astype(F32)
    spread = jnp.concatenate([query[i : i + 1] * mine for i in range(rows)], axis=0).astype(BF16)
    scores = dot_nt(spread, keys) * (1.0 / math.sqrt(head_size)) + bias[...].reshape(
        rows * heads, tokens
    )
    live = flags[...] == 1
    scores = jnp.where(live, scores, -1e30)
    peak = jnp.max(scores, axis=-1, keepdims=True)
    expos = jnp.where(live, jnp.exp(scores - peak), 0.0)
    sums = jnp.sum(expos, axis=-1, keepdims=True)
    blended = dot(expos.astype(BF16), values) / sums
    attended = jnp.concatenate(
        [
            jnp.sum(blended[i * heads : (i + 1) * heads] * mine, axis=0, keepdims=True)
            for i in range(rows)
        ],
        axis=0,
    )
    attended = (attended * gate).astype(BF16)
    single_out[...] = (residue[...].astype(F32) + dot(attended, merge[...])).astype(BF16)
    for copy in started:
        copy.wait_send()


def local(
    sequence_features,
    edge_features,
    residue_features,
    polymer_labels,
    polymer_membership,
    present_residue_flags,
    sequence_scaling_vector,
    first_embedding_matrix,
    second_embedding_matrix,
    contraction_matrix,
    contraction_offset,
    feedforward_scaling_vector,
    feedforward_switch_matrix,
    widening_matrix,
    narrowing_matrix,
    logit_scaling_vector,
    edge_logit_matrix,
    residue_scaling_vector,
    asking_matrix,
    lookup_matrix,
    content_matrix,
    heads_sigmoid_matrix,
    heads_merge_matrix,
):
    entries, rows, _ = sequence_features.shape
    tokens, width = edge_features.shape[1:]
    factors = first_embedding_matrix.shape[1]
    heads = edge_logit_matrix.shape[1]
    count = lax.axis_size("row")
    slow, fast, core = digits(count)
    sends = (slow - 1) + slow * (fast - 1) + (slow * fast if core == 2 else 0)
    layers = factors + residue_features.shape[1] // entries
    arrays = (
        sequence_features.transpose(1, 2, 0),
        edge_features,
        residue_features,
        polymer_labels[None],
        polymer_membership,
        present_residue_flags[None],
        sequence_scaling_vector[None],
        first_embedding_matrix.T,
        second_embedding_matrix.T,
        contraction_matrix,
        contraction_offset[None],
        feedforward_scaling_vector[None],
        feedforward_switch_matrix,
        widening_matrix,
        narrowing_matrix,
        logit_scaling_vector[None],
        edge_logit_matrix.T,
        residue_scaling_vector,
        asking_matrix,
        lookup_matrix,
        content_matrix,
        heads_sigmoid_matrix,
        heads_merge_matrix,
    )
    large = (1, 9, 12, 13, 14, 18, 19, 20, 21, 22)
    return pl.pallas_call(
        functools.partial(kernel, count),
        out_shape=(
            jax.ShapeDtypeStruct(edge_features.shape, edge_features.dtype),
            jax.ShapeDtypeStruct(residue_features.shape, residue_features.dtype),
        ),
        in_specs=[
            pl.BlockSpec(memory_space=pl.ANY if index in large else pltpu.VMEM)
            for index in range(len(arrays))
        ],
        out_specs=(pl.BlockSpec(memory_space=pltpu.VMEM),) * 2,
        scratch_shapes=[
            pltpu.VMEM((factors, rows, entries), F32),
            pltpu.VMEM((rows, entries, factors), BF16),
            pltpu.VMEM(contraction_matrix.shape, F32),
            pltpu.VMEM(arrays[1].shape, BF16),
            pltpu.VMEM(arrays[9].shape, BF16),
            pltpu.VMEM(arrays[12].shape, BF16),
            pltpu.VMEM(arrays[13].shape, BF16),
            pltpu.VMEM(arrays[14].shape, BF16),
            pltpu.VMEM(arrays[18].shape, BF16),
            pltpu.VMEM(arrays[19].shape, BF16),
            pltpu.VMEM(arrays[20].shape, BF16),
            pltpu.VMEM(arrays[21].shape, BF16),
            pltpu.VMEM(arrays[22].shape, BF16),
            pltpu.VMEM((layers, rows, entries), BF16),
            pltpu.VMEM((count, layers, rows, entries), BF16),
            pltpu.VMEM((factors * entries, rows * width), BF16),
            pltpu.VMEM((tokens, layers * entries), BF16),
            pltpu.VMEM((rows, heads, tokens), F32),
            pltpu.VMEM((tokens, rows), F32),
            pltpu.SemaphoreType.DMA((sends,)),
            pltpu.SemaphoreType.DMA((count,)),
            pltpu.SemaphoreType.DMA((len(large),)),
        ],
        compiler_params=pltpu.CompilerParams(
            collective_id=0, has_side_effects=True, vmem_limit_bytes=56 * 2**20
        ),
        name="trunk",
    )(*arrays)


def solution(mesh):
    placed = (
        P("grp", "row", None),
        P(("grp", "row"), None, None),
        P(("grp", "row"), None),
        P("grp"),
        P("grp", None),
        P("grp"),
        P(),
        P(),
        P(),
        P(),
        P(),
        P(),
        P(),
        P(),
        P(),
        P(),
        P(),
        P(),
        P(),
        P(),
        P(),
        P(),
        P(),
    )
    return jax.shard_map(
        local,
        mesh=mesh,
        in_specs=placed,
        out_specs=(P(("grp", "row"), None, None), P(("grp", "row"), None)),
        check_vma=False,
    )
```
